256 devices in a mesh: dp: 32 (over z, y_hi, core), node: 8 (over x, y_lo).
Axes of the slice: x: 4, y: 4 (y_hi: 2, y_lo: 2; y = y_hi * 2 + y_lo), z: 8, core: 2. Of those that a mesh axis runs over, the one named last changes fastest.
Arguments:
- tokens: bfloat16 [1024, 8192], P('dp', 'node'), may hold values from -6 to 6
- grad_out: bfloat16 [1024, 8192], P('dp', 'node'), may hold values from -6 to 6
- w_in: bfloat16 [8192, 32768], P('node', 'dp'), may hold values from -0.0625 to 0.0625
- w_out: bfloat16 [32768, 8192], P('dp', 'node'), may hold values from -0.0625 to 0.0625
Outputs:
- grad_in: bfloat16 [1024, 8192], P('dp', 'node')
- grad_w_in: float32 [8192, 32768], P('node', 'dp')
- grad_w_out: float32 [32768, 8192], P('dp', 'node')
The draws below stay inside these ranges and needn't reach their ends.
All inputs are finite; a program needn't handle non-finite values.
Results may differ from the reference program's by a relative error of at most 0.0049.
Values may be sent and summed in bfloat16 or wider, within the bound.
No kernel may reach another device: no remote copies, remote signals or barrier semaphores. Data moves between devices by JAX's collectives and lax.ppermute only.
A program may use at most 64 MiB of HBM per device.

```python
import math
import jax
import jax.numpy as jnp

D = 8192
FW = 32768
TOKENS = 1024


def block_scale(rng, extent, cuts, low, top_value):
    def one(dim, blocks):
        heights = jax.random.uniform(jax.random.fold_in(jax.random.fold_in(rng, 6), dim), (blocks,), jnp.float32, low / len(cuts), top_value / len(cuts))
        return jnp.repeat(jnp.exp(heights), extent[dim] // blocks).reshape((-1,) + (1,) * (len(extent) - dim - 1))

    loudness = one(*cuts[0])
    for cut in cuts[1:]:
        loudness = loudness * one(*cut)
    return loudness


def normal_values(key, dims, width, limit, shards=(), held_as=jnp.bfloat16):
    result = width * jax.random.normal(key, dims, jnp.float32)
    if shards:
        result = result * block_scale(key, dims, shards, -0.22, 0.18)
    return jnp.clip(result, -limit, limit).astype(held_as)


def setup_inputs(seed: int = 0) -> dict:
    streams_of = jax.random.split(jax.random.key(seed), 5)
    tokens = normal_values(streams_of[0], (TOKENS, D), 1.0, 6.0, ((0, 32), (1, 8)))
    grad_out = normal_values(streams_of[1], (TOKENS, D), 1.0, 6.0, ((0, 32), (1, 8)))
    w_in = normal_values(streams_of[2], (D, FW), D ** -0.5, 0.0625, ((0, 8), (1, 32)))
    w_out = normal_values(streams_of[3], (FW, D), D ** -0.5, 0.0625, ((0, 32), (1, 8)))
    return {"tokens": tokens, "grad_out": grad_out, "w_in": w_in, "w_out": w_out}


def reference(tokens, grad_out, w_in, w_out):
    scale = 1.0 / math.sqrt(TOKENS)
    preact = jnp.dot(tokens, w_in, preferred_element_type=jnp.float32)
    normal_cdf = 0.5 * (1.0 + jax.scipy.special.erf(preact / jnp.sqrt(jnp.float32(2.0))))
    normal_pdf = jnp.exp(-0.5 * preact * preact) / jnp.sqrt(jnp.float32(2.0 * 3.141592653589793))
    activated = (preact * normal_cdf).astype(jnp.bfloat16)
    back_grad = jnp.dot(grad_out, w_out.T, preferred_element_type=jnp.float32)
    slopes = (back_grad * (normal_cdf + preact * normal_pdf)).astype(jnp.bfloat16)
    grad_in = jnp.dot(slopes, w_in.T, preferred_element_type=jnp.float32).astype(jnp.bfloat16)
    grad_w_in = jnp.dot(tokens.T, slopes, preferred_element_type=jnp.float32) * scale
    grad_w_out = jnp.dot(activated.T, grad_out, preferred_element_type=jnp.float32) * scale
    return (grad_in, grad_w_in, grad_w_out)
```

```python
import math

import jax
import jax.numpy as jnp
from jax import lax
from jax.sharding import Mesh, PartitionSpec as P

SIZES = {"z": 8, "yh": 2, "core": 2, "x": 4, "yl": 2}
DP = ("z", "yh", "core")
NODE = ("x", "yl")
BLOCK_OF = {0: (0, 0), 4: (0, 1), 1: (1, 0), -1: (1, 1), 2: (2, 0), -2: (2, 1), 3: (3, 0), -3: (3, 1)}


def move(value, axis, step=1):
    n = SIZES[axis]
    return lax.ppermute(value, axis, [(i, (i + step) % n) for i in range(n)])


def send_home(value, r, side):
    distance = {where: d for d, where in BLOCK_OF.items()}
    pairs = []
    for z in range(8):
        for x in range(4):
            to = (z + distance[(x + r) % 4, side]) % 8
            pairs.append((z * 4 + x, to * 4 + x))
    return lax.ppermute(value, ("z", "x"), pairs)


def gelu_parts(preact, back_grad):
    normal_cdf = 0.5 * (1.0 + jax.scipy.special.erf(preact / jnp.sqrt(jnp.float32(2.0))))
    normal_pdf = jnp.exp(-0.5 * preact * preact) / jnp.sqrt(jnp.float32(2.0 * 3.141592653589793))
    activated = (preact * normal_cdf).astype(jnp.bfloat16)
    slopes = (back_grad * (normal_cdf + preact * normal_pdf)).astype(jnp.bfloat16)
    return (activated, slopes)


def f32(v):
    return v.astype(jnp.float32)


def bf16(v):
    return v.astype(jnp.bfloat16)


def at(value, axis, index):
    return lax.dynamic_index_in_dim(value, index, axis, keepdims=False)


def after(first, then):
    return lax.optimization_barrier((first, then))[1]


def widen(half, side):
    spread = [(0, 0, 0)] * (half.ndim + 1)
    spread[-3] = (side, 1 - side, 0)
    return lax.pad(jnp.expand_dims(f32(half), -3), jnp.float32(0), spread)


def times_in(rows, w_in):
    return jnp.dot(rows.reshape(-1, 1024), w_in, preferred_element_type=jnp.float32)


def times_out(rows, w_out):
    return lax.dot_general(
        rows.reshape(-1, 1024), w_out, (((1,), (1,)), ((), ())), preferred_element_type=jnp.float32
    )


def body(tokens, grad_out, w_in, w_out):
    scale = 1.0 / math.sqrt(1024)
    x, yl = lax.axis_index("x"), lax.axis_index("yl")
    own = jnp.stack([tokens, grad_out])
    own = jnp.concatenate([own, move(own, "yh")], axis=1)

    rows = jnp.zeros((2, 4, 2, 2, 64, 1024), jnp.bfloat16)

    def put(rows, value, d, start=0):
        block, side = BLOCK_OF[d]
        for core, v in ((0, value), (1, move(value, "core"))):
            v = v.reshape(2, 1, 1, 1, -1, 1024)
            rows = lax.dynamic_update_slice(rows, v, (0, block, core, side, start, 0))
        return rows

    rows = put(rows, own, 0)
    up, down = own, own
    for k in (1, 2, 3):
        up, down = move(up, "z", 1), move(down, "z", -1)
        rows = put(rows, up, -k)
        rows = put(rows, down, k)
    up, down = move(up[:, :32], "z", 1), move(down[:, 32:], "z", -1)
    rows = put(rows, up, 4, 0)
    rows = put(rows, down, 4, 32)
    toks = rows[0].reshape(4, 2, 128, 1024)
    grads = rows[1].reshape(4, 2, 128, 1024)

    far = bf16(times_in(at(toks, 0, (x + 2) % 4), w_in)).reshape(2, 128, 1024)
    up, down = move(far[0], "x", 1), move(far[1], "x", -1)
    leave = bf16(times_out(at(grads, 1, 1 - yl), w_out))
    got = move(leave, "yl").reshape(4, 128, 1024)
    one = times_in(at(toks, 0, (x + 1) % 4), w_in).reshape(2, 128, 1024)
    three = times_in(at(toks, 0, (x + 3) % 4), w_in).reshape(2, 128, 1024)
    one = move(bf16(one + widen(up, 0)), "x", 1)
    three = move(bf16(three + widen(down, 1)), "x", -1)
    mine = times_in(at(toks, 0, x), w_in).reshape(2, 128, 1024)
    other = bf16(at(mine, 0, 1 - yl) + f32(at(one, 0, 1 - yl)) + f32(at(three, 0, 1 - yl)))
    other = move(other, "yl")
    preact = at(mine, 0, yl) + f32(at(one, 0, yl)) + f32(at(three, 0, yl)) + f32(other)

    back = times_out(at(grads, 1, yl), w_out).reshape(4, 128, 1024)
    sends = [bf16(at(back, 0, (x + r) % 4) + f32(at(got, 0, (x + r) % 4))) for r in (2, 1, 3)]
    sends = [f32(move(v, "x", r)) for r, v in zip((2, 1, 3), sends)]
    back_grad = at(back, 0, x) + f32(at(got, 0, x)) + sends[0] + sends[1] + sends[2]

    act, slopes = gelu_parts(preact, back_grad)

    def spread(own, earlier=None):
        other = move(own, "yl")
        pair = jnp.where(yl == 0, jnp.stack([own, other]), jnp.stack([other, own]))
        if earlier is not None:
            pair = after(earlier, pair)
        below, above = move(pair, "x", 1), move(pair, "x", -1)
        far = jnp.stack([move(below[0], "x", 1), move(above[1], "x", -1)])
        blocks = {0: pair, 1: above, 3: below, 2: far}
        out = jnp.zeros((4, 2, 128, 1024), jnp.bfloat16)
        for r, block in blocks.items():
            out = lax.dynamic_update_index_in_dim(out, block, (x + r) % 4, 0)
        return blocks, out.reshape(1024, 1024)

    blocks, slopes = spread(slopes)
    total = None
    for r in (0, 1, 3, 2):
        g_in = lax.dot_general(
            blocks[r].reshape(256, 1024), w_in, (((1,), (1,)), ((), ())),
            preferred_element_type=jnp.float32,
        ).reshape(2, 2, 64, 1024)
        g_in = bf16(g_in[0] + move(g_in[1], "core"))
        if r in (1, 3):
            g_in = after(first, g_in)
        back_home = f32(send_home(g_in[0], r, 0)) + f32(send_home(g_in[1], r, 1))
        total = back_home if total is None else total + back_home
        if r == 0:
            first = total
    grad_in = bf16(total[:32] + move(total[32:], "yh"))
    grad_w_in = lax.dot_general(
        toks.reshape(1024, 1024), slopes, (((0,), (0,)), ((), ())), preferred_element_type=jnp.float32
    )
    _, act = spread(act, blocks[2])
    grad_w_out = lax.dot_general(
        act, grads.reshape(1024, 1024), (((0,), (0,)), ((), ())), preferred_element_type=jnp.float32
    )
    return (grad_in, grad_w_in * scale, grad_w_out * scale)


def solution(mesh):
    fine = Mesh(mesh.devices.reshape(8, 2, 2, 4, 2), DP + NODE)
    in_specs = (P(DP, NODE), P(DP, NODE), P(NODE, DP), P(DP, NODE))
    out_specs = (P(DP, NODE), P(NODE, DP), P(DP, NODE))
    return jax.shard_map(body, mesh=fine, in_specs=in_specs, out_specs=out_specs, check_vma=False)
```

```python
import math

import jax
import jax.numpy as jnp
from jax import lax
from jax.sharding import Mesh, PartitionSpec as P

SIZES = {"z": 8, "yh": 2, "core": 2, "x": 4, "yl": 2}
DP = ("z", "yh", "core")
NODE = ("x", "yl")
BLOCK_OF = {0: (0, 0), 4: (0, 1), 1: (1, 0), -1: (1, 1), 2: (2, 0), -2: (2, 1), 3: (3, 0), -3: (3, 1)}


def move(value, axis, step=1):
    n = SIZES[axis]
    return lax.ppermute(value, axis, [(i, (i + step) % n) for i in range(n)])


def send_home(value, r, side):
    distance = {where: d for d, where in BLOCK_OF.items()}
    pairs = []
    for z in range(8):
        for x in range(4):
            to = (z + distance[(x + r) % 4, side]) % 8
            pairs.append((z * 4 + x, to * 4 + x))
    return lax.ppermute(value, ("z", "x"), pairs)


def gelu_parts(preact, back_grad):
    normal_cdf = 0.5 * (1.0 + jax.scipy.special.erf(preact / jnp.sqrt(jnp.float32(2.0))))
    normal_pdf = jnp.exp(-0.5 * preact * preact) / jnp.sqrt(jnp.float32(2.0 * 3.141592653589793))
    activated = (preact * normal_cdf).astype(jnp.bfloat16)
    slopes = (back_grad * (normal_cdf + preact * normal_pdf)).astype(jnp.bfloat16)
    return (activated, slopes)


def f32(v):
    return v.astype(jnp.float32)


def bf16(v):
    return v.astype(jnp.bfloat16)


def at(value, axis, index):
    return lax.dynamic_index_in_dim(value, index, axis, keepdims=False)


def after(first, then):
    zero = jnp.minimum(jnp.abs(first[(0,) * first.ndim]), 0)
    return then + zero.astype(then.dtype)


def widen(half, side):
    spread = [(0, 0, 0)] * (half.ndim + 1)
    spread[-3] = (side, 1 - side, 0)
    return lax.pad(jnp.expand_dims(f32(half), -3), jnp.float32(0), spread)


def times_in(rows, w_in):
    return jnp.dot(rows.reshape(-1, 1024), w_in, preferred_element_type=jnp.float32)


def times_out(rows, w_out):
    return lax.dot_general(
        rows.reshape(-1, 1024), w_out, (((1,), (1,)), ((), ())), preferred_element_type=jnp.float32
    )


def body(tokens, grad_out, w_in, w_out):
    scale = 1.0 / math.sqrt(1024)
    x, yl = lax.axis_index("x"), lax.axis_index("yl")
    own = jnp.stack([tokens, grad_out])
    own = jnp.concatenate([own, move(own, "yh")], axis=1)

    rows = jnp.zeros((2, 4, 2, 2, 64, 1024), jnp.bfloat16)

    def put(rows, value, d, start=0):
        block, side = BLOCK_OF[d]
        other = move(value, "core")
        for core, v in ((0, value), (1, other)):
            v = v.reshape(2, 1, 1, 1, -1, 1024)
            rows = lax.dynamic_update_slice(rows, v, (0, block, core, side, start, 0))
        return rows, (value, other)

    def leave(pieces):
        mine = jnp.concatenate([jnp.where(yl == 0, o[1], v[1]) for v, o in pieces], axis=0)
        return move(bf16(times_out(mine, w_out)), "yl").reshape(2, 128, 1024)

    rows, held = put(rows, own, 0)
    up, down = own, own
    held = {0: held}
    for k in (1, 2, 3):
        up, down = move(up, "z", 1), move(down, "z", -1)
        rows, held[-k] = put(rows, up, -k)
        rows, held[k] = put(rows, down, k)
        if k == 2:
            got = leave([held[d] for d in (1, -1, 2, -2)])
    up, down = move(up[:, :32], "z", 1), move(down[:, 32:], "z", -1)
    rows, above = put(rows, up, 4, 0)
    rows, below = put(rows, down, 4, 32)
    got = jnp.concatenate([got, leave([held[3], held[-3], held[0], above, below])], axis=0)
    toks = rows[0].reshape(4, 2, 128, 1024)
    grads = rows[1].reshape(4, 2, 128, 1024)

    far = bf16(times_in(at(toks, 0, (x + 2) % 4), w_in)).reshape(2, 128, 1024)
    up, down = move(far[0], "x", 1), move(far[1], "x", -1)
    one = times_in(at(toks, 0, (x + 1) % 4), w_in).reshape(2, 128, 1024)
    three = times_in(at(toks, 0, (x + 3) % 4), w_in).reshape(2, 128, 1024)
    one = move(bf16(one + widen(up, 0)), "x", 1)
    three = move(bf16(three + widen(down, 1)), "x", -1)
    mine = times_in(at(toks, 0, x), w_in).reshape(2, 128, 1024)
    other = bf16(at(mine, 0, 1 - yl) + f32(at(one, 0, 1 - yl)) + f32(at(three, 0, 1 - yl)))
    other = move(other, "yl")
    preact = at(mine, 0, yl) + f32(at(one, 0, yl)) + f32(at(three, 0, yl)) + f32(other)

    back = times_out(at(grads, 1, yl), w_out).reshape(4, 128, 1024)
    sends = [bf16(at(back, 0, (x + r) % 4) + f32(at(got, 0, (x + r + 3) % 4))) for r in (2, 1, 3)]
    sends = [f32(move(v, "x", r)) for r, v in zip((2, 1, 3), sends)]
    back_grad = at(back, 0, x) + f32(at(got, 0, (x + 3) % 4)) + sends[0] + sends[1] + sends[2]

    act, slopes = gelu_parts(preact, back_grad)

    def begin(own):
        other = move(own, "yl")
        pair = jnp.where(yl == 0, jnp.stack([own, other]), jnp.stack([other, own]))
        return pair, move(pair, "x", -1), move(pair, "x", 1)

    def end(pair, above, below, first=None):
        up, down = below[0], above[1]
        if first is not None:
            up, down = after(first, up), after(first, down)
        far = jnp.stack([move(up, "x", 1), move(down, "x", -1)])
        out = jnp.zeros((4, 2, 128, 1024), jnp.bfloat16)
        for r, block in ((0, pair), (1, above), (3, below), (2, far)):
            out = lax.dynamic_update_index_in_dim(out, block, (x + r) % 4, 0)
        return far, out.reshape(1024, 1024)

    pair, above, below = begin(slopes)
    far, slopes = end(pair, above, below)
    total = None
    for r, block in ((0, pair), (1, above), (3, below), (2, far)):
        g_in = lax.dot_general(
            block.reshape(256, 1024), w_in, (((1,), (1,)), ((), ())), preferred_element_type=jnp.float32
        ).reshape(2, 2, 64, 1024)
        g_in = bf16(g_in[0] + move(g_in[1], "core"))
        back_home = f32(send_home(g_in[0], r, 0)) + f32(send_home(g_in[1], r, 1))
        total = back_home if total is None else total + back_home
    _, act = end(*begin(act), g_in)
    grad_in = bf16(total[:32] + move(total[32:], "yh"))
    grad_w_in = lax.dot_general(
        toks.reshape(1024, 1024), slopes, (((0,), (0,)), ((), ())), preferred_element_type=jnp.float32
    )
    grad_w_out = lax.dot_general(
        act, grads.reshape(1024, 1024), (((0,), (0,)), ((), ())), preferred_element_type=jnp.float32
    )
    return (grad_in, grad_w_in * scale, grad_w_out * scale)


def solution(mesh):
    fine = Mesh(mesh.devices.reshape(8, 2, 2, 4, 2), DP + NODE)
    in_specs = (P(DP, NODE), P(DP, NODE), P(NODE, DP), P(DP, NODE))
    out_specs = (P(DP, NODE), P(NODE, DP), P(DP, NODE))
    return jax.shard_map(body, mesh=fine, in_specs=in_specs, out_specs=out_specs, check_vma=False)
```

```python
import math

import jax
import jax.numpy as jnp
from jax import lax
from jax.sharding import Mesh, PartitionSpec as P

SIZES = {"z": 8, "yh": 2, "core": 2, "x": 4, "yl": 2}
DP = ("z", "yh", "core")
NODE = ("x", "yl")
BLOCK_OF = {0: (0, 0), 4: (0, 1), 1: (1, 0), -1: (1, 1), 2: (2, 0), -2: (2, 1), 3: (3, 0), -3: (3, 1)}


def move(value, axis, step=1):
    n = SIZES[axis]
    return lax.ppermute(value, axis, [(i, (i + step) % n) for i in range(n)])


def send_home(value, r, side):
    distance = {where: d for d, where in BLOCK_OF.items()}
    pairs = []
    for z in range(8):
        for x in range(4):
            to = (z + distance[(x + r) % 4, side]) % 8
            pairs.append((z * 4 + x, to * 4 + x))
    return lax.ppermute(value, ("z", "x"), pairs)


def gelu_parts(preact, back_grad):
    normal_cdf = 0.5 * (1.0 + jax.scipy.special.erf(preact / jnp.sqrt(jnp.float32(2.0))))
    normal_pdf = jnp.exp(-0.5 * preact * preact) / jnp.sqrt(jnp.float32(2.0 * 3.141592653589793))
    activated = (preact * normal_cdf).astype(jnp.bfloat16)
    slopes = (back_grad * (normal_cdf + preact * normal_pdf)).astype(jnp.bfloat16)
    return (activated, slopes)


def f32(v):
    return v.astype(jnp.float32)


def bf16(v):
    return v.astype(jnp.bfloat16)


def at(value, axis, index):
    return lax.dynamic_index_in_dim(value, index, axis, keepdims=False)


def after(first, then):
    zero = jnp.minimum(jnp.abs(first[(0,) * first.ndim]), 0)
    return then + zero.astype(then.dtype)


def widen(half, side):
    spread = [(0, 0, 0)] * (half.ndim + 1)
    spread[-3] = (side, 1 - side, 0)
    return lax.pad(jnp.expand_dims(f32(half), -3), jnp.float32(0), spread)


def times_in(rows, w_in):
    return jnp.dot(rows.reshape(-1, 1024), w_in, preferred_element_type=jnp.float32)


def times_out(rows, w_out):
    return lax.dot_general(
        rows.reshape(-1, 1024), w_out, (((1,), (1,)), ((), ())), preferred_element_type=jnp.float32
    )


def body(tokens, grad_out, w_in, w_out):
    scale = 1.0 / math.sqrt(1024)
    x, yl = lax.axis_index("x"), lax.axis_index("yl")
    own = jnp.stack([tokens, grad_out])
    own = jnp.concatenate([own, move(own, "yh")], axis=1)

    rows = jnp.zeros((2, 4, 2, 2, 64, 1024), jnp.bfloat16)

    def put(rows, value, d, start=0):
        block, side = BLOCK_OF[d]
        other = move(value, "core")
        for core, v in ((0, value), (1, other)):
            v = v.reshape(2, 1, 1, 1, -1, 1024)
            rows = lax.dynamic_update_slice(rows, v, (0, block, core, side, start, 0))
        return rows, (value, other)

    def leave(pieces):
        mine = jnp.concatenate([jnp.where(yl == 0, o[1], v[1]) for v, o in pieces], axis=0)
        return bf16(times_out(mine, w_out)).reshape(2, 128, 1024)

    rows, held = put(rows, own, 0)
    up, down = own, own
    held = {0: held}
    for k in (1, 2, 3):
        up, down = move(up, "z", 1), move(down, "z", -1)
        rows, held[-k] = put(rows, up, -k)
        rows, held[k] = put(rows, down, k)
        if k == 2:
            early = leave([held[d] for d in (1, -1, 2, -2)])
    up, down = move(after(early, up[:, :32]), "z", 1), move(after(early, down[:, 32:]), "z", -1)
    rows, above = put(rows, up, 4, 0)
    rows, below = put(rows, down, 4, 32)
    late = leave([held[3], held[-3], held[0], above, below])
    got = jnp.concatenate([move(early, "yl"), move(late, "yl")], axis=0)
    toks = rows[0].reshape(4, 2, 128, 1024)
    grads = rows[1].reshape(4, 2, 128, 1024)

    far = bf16(times_in(at(toks, 0, (x + 2) % 4), w_in)).reshape(2, 128, 1024)
    up, down = move(far[0], "x", 1), move(far[1], "x", -1)
    one = times_in(at(toks, 0, (x + 1) % 4), w_in).reshape(2, 128, 1024)
    three = times_in(at(toks, 0, (x + 3) % 4), w_in).reshape(2, 128, 1024)
    one = move(bf16(one + widen(up, 0)), "x", 1)
    three = move(bf16(three + widen(down, 1)), "x", -1)
    mine = times_in(at(toks, 0, x), w_in).reshape(2, 128, 1024)
    other = bf16(at(mine, 0, 1 - yl) + f32(at(one, 0, 1 - yl)) + f32(at(three, 0, 1 - yl)))
    other = move(other, "yl")
    preact = at(mine, 0, yl) + f32(at(one, 0, yl)) + f32(at(three, 0, yl)) + f32(other)

    back = times_out(at(grads, 1, yl), w_out).reshape(4, 128, 1024)
    sends = [bf16(at(back, 0, (x + r) % 4) + f32(at(got, 0, (x + r + 3) % 4))) for r in (2, 1, 3)]
    sends = [f32(move(v, "x", r)) for r, v in zip((2, 1, 3), sends)]
    back_grad = at(back, 0, x) + f32(at(got, 0, (x + 3) % 4)) + sends[0] + sends[1] + sends[2]

    act, slopes = gelu_parts(preact, back_grad)

    def begin(own):
        other = move(own, "yl")
        pair = jnp.where(yl == 0, jnp.stack([own, other]), jnp.stack([other, own]))
        return pair, move(pair, "x", -1), move(pair, "x", 1)

    def end(pair, above, below, first=None):
        up, down = below[0], above[1]
        if first is not None:
            up, down = after(first, up), after(first, down)
        far = jnp.stack([move(up, "x", 1), move(down, "x", -1)])
        out = jnp.zeros((4, 2, 128, 1024), jnp.bfloat16)
        for r, block in ((0, pair), (1, above), (3, below), (2, far)):
            out = lax.dynamic_update_index_in_dim(out, block, (x + r) % 4, 0)
        return far, out.reshape(1024, 1024)

    pair, above, below = begin(slopes)
    far, slopes = end(pair, above, below)
    total = None
    for r, block in ((0, pair), (1, above), (3, below), (2, far)):
        g_in = lax.dot_general(
            block.reshape(256, 1024), w_in, (((1,), (1,)), ((), ())), preferred_element_type=jnp.float32
        ).reshape(2, 2, 64, 1024)
        g_in = bf16(g_in[0] + move(g_in[1], "core"))
        back_home = f32(send_home(g_in[0], r, 0)) + f32(send_home(g_in[1], r, 1))
        total = back_home if total is None else total + back_home
    _, act = end(*begin(act), g_in)
    grad_in = bf16(total[:32] + move(total[32:], "yh"))
    grad_w_in = lax.dot_general(
        toks.reshape(1024, 1024), slopes, (((0,), (0,)), ((), ())), preferred_element_type=jnp.float32
    )
    grad_w_out = lax.dot_general(
        act, grads.reshape(1024, 1024), (((0,), (0,)), ((), ())), preferred_element_type=jnp.float32
    )
    return (grad_in, grad_w_in * scale, grad_w_out * scale)


def solution(mesh):
    fine = Mesh(mesh.devices.reshape(8, 2, 2, 4, 2), DP + NODE)
    in_specs = (P(DP, NODE), P(DP, NODE), P(NODE, DP), P(DP, NODE))
    out_specs = (P(DP, NODE), P(NODE, DP), P(DP, NODE))
    return jax.shard_map(body, mesh=fine, in_specs=in_specs, out_specs=out_specs, check_vma=False)
```

```python
import math

import jax
import jax.numpy as jnp
from jax import lax
from jax.sharding import Mesh, PartitionSpec as P

SIZES = {"z": 8, "yh": 2, "core": 2, "x": 4, "yl": 2}
DP = ("z", "yh", "core")
NODE = ("x", "yl")
BLOCK_OF = {0: (0, 0), 4: (0, 1), 1: (1, 0), -1: (1, 1), 2: (2, 0), -2: (2, 1), 3: (3, 0), -3: (3, 1)}


def move(value, axis, step=1):
    n = SIZES[axis]
    return lax.ppermute(value, axis, [(i, (i + step) % n) for i in range(n)])


def send_home(value, r, side):
    distance = {where: d for d, where in BLOCK_OF.items()}
    pairs = []
    for z in range(8):
        for x in range(4):
            to = (z + distance[(x + r) % 4, side]) % 8
            pairs.append((z * 4 + x, to * 4 + x))
    return lax.ppermute(value, ("z", "x"), pairs)


def gelu_parts(preact, back_grad):
    normal_cdf = 0.5 * (1.0 + jax.scipy.special.erf(preact / jnp.sqrt(jnp.float32(2.0))))
    normal_pdf = jnp.exp(-0.5 * preact * preact) / jnp.sqrt(jnp.float32(2.0 * 3.141592653589793))
    activated = (preact * normal_cdf).astype(jnp.bfloat16)
    slopes = (back_grad * (normal_cdf + preact * normal_pdf)).astype(jnp.bfloat16)
    return (activated, slopes)


def f32(v):
    return v.astype(jnp.float32)


def bf16(v):
    return v.astype(jnp.bfloat16)


def at(value, axis, index):
    return lax.dynamic_index_in_dim(value, index, axis, keepdims=False)


def after(first, then):
    zero = jnp.minimum(jnp.abs(first[(0,) * first.ndim]), 0)
    return then + zero.astype(then.dtype)


def widen(half, side):
    spread = [(0, 0, 0)] * (half.ndim + 1)
    spread[-3] = (side, 1 - side, 0)
    return lax.pad(jnp.expand_dims(f32(half), -3), jnp.float32(0), spread)


def times_in(rows, w_in):
    return jnp.dot(rows.reshape(-1, 1024), w_in, preferred_element_type=jnp.float32)


def times_out(rows, w_out):
    return lax.dot_general(
        rows.reshape(-1, 1024), w_out, (((1,), (1,)), ((), ())), preferred_element_type=jnp.float32
    )


def body(tokens, grad_out, w_in, w_out):
    scale = 1.0 / math.sqrt(1024)
    x, yl = lax.axis_index("x"), lax.axis_index("yl")
    own = jnp.stack([tokens, grad_out])

    rows = jnp.zeros((2, 4, 2, 2, 64, 1024), jnp.bfloat16)

    def complete(value):
        value = jnp.concatenate([value, move(value, "yh")], axis=2)
        return value, move(value, "core")

    def put(rows, pieces, block, side):
        for core, v in enumerate(pieces):
            rows = lax.dynamic_update_slice(rows, v[:, None, None], (0, block, core, side, 0, 0))
        return rows

    def leave(pieces):
        mine = [jnp.where(yl == 0, o[1], v[1]).reshape(-1, 1024) for v, o in pieces]
        return move(bf16(times_out(jnp.concatenate(mine, axis=0), w_out)), "yl").reshape(2, 128, 1024)

    held = {0: complete(own[:, None])}
    rows = put(rows, held[0], 0, 0)
    up, down = own, own
    for k in (1, 2, 3):
        up, down = move(up, "z", 1), move(down, "z", -1)
        held[k] = complete(jnp.stack([down, up], axis=1))
        rows = put(rows, held[k], k, 0)
        if k == 2:
            got = leave([held[1], held[2]])
    up, down = move(up[:, :16], "z", 1), move(down[:, 16:], "z", -1)
    held[4] = complete(jnp.concatenate([up, down], axis=1)[:, None])
    rows = put(rows, held[4], 0, 1)
    got = jnp.concatenate([got, leave([held[3], held[0], held[4]])], axis=0)
    toks = rows[0].reshape(4, 2, 128, 1024)
    grads = rows[1].reshape(4, 2, 128, 1024)

    far = bf16(times_in(at(toks, 0, (x + 2) % 4), w_in)).reshape(2, 128, 1024)
    up, down = move(far[0], "x", 1), move(far[1], "x", -1)
    one = times_in(at(toks, 0, (x + 1) % 4), w_in).reshape(2, 128, 1024)
    three = times_in(at(toks, 0, (x + 3) % 4), w_in).reshape(2, 128, 1024)
    one = move(bf16(one + widen(up, 0)), "x", 1)
    three = move(bf16(three + widen(down, 1)), "x", -1)
    mine = times_in(at(toks, 0, x), w_in).reshape(2, 128, 1024)
    other = bf16(at(mine, 0, 1 - yl) + f32(at(one, 0, 1 - yl)) + f32(at(three, 0, 1 - yl)))
    other = move(other, "yl")
    preact = at(mine, 0, yl) + f32(at(one, 0, yl)) + f32(at(three, 0, yl)) + f32(other)

    back = times_out(at(grads, 1, yl), w_out).reshape(4, 128, 1024)
    sends = [bf16(at(back, 0, (x + r) % 4) + f32(at(got, 0, (x + r + 3) % 4))) for r in (2, 1, 3)]
    sends = [f32(move(v, "x", r)) for r, v in zip((2, 1, 3), sends)]
    back_grad = at(back, 0, x) + f32(at(got, 0, (x + 3) % 4)) + sends[0] + sends[1] + sends[2]

    act, slopes = gelu_parts(preact, back_grad)

    def begin(own):
        other = move(own, "yl")
        pair = jnp.where(yl == 0, jnp.stack([own, other]), jnp.stack([other, own]))
        return pair, move(pair, "x", -1), move(pair, "x", 1)

    def end(pair, above, below, first=None):
        up, down = below[0], above[1]
        if first is not None:
            up, down = after(first, up), after(first, down)
        far = jnp.stack([move(up, "x", 1), move(down, "x", -1)])
        out = jnp.zeros((4, 2, 128, 1024), jnp.bfloat16)
        for r, block in ((0, pair), (1, above), (3, below), (2, far)):
            out = lax.dynamic_update_index_in_dim(out, block, (x + r) % 4, 0)
        return far, out.reshape(1024, 1024)

    pair, above, below = begin(slopes)
    far, slopes = end(pair, above, below)
    total = None
    for r, block in ((0, pair), (1, above), (3, below), (2, far)):
        g_in = lax.dot_general(
            block.reshape(256, 1024), w_in, (((1,), (1,)), ((), ())), preferred_element_type=jnp.float32
        ).reshape(2, 2, 64, 1024)
        g_in = bf16(g_in[0] + move(g_in[1], "core"))
        back_home = f32(send_home(g_in[0], r, 0)) + f32(send_home(g_in[1], r, 1))
        total = back_home if total is None else total + back_home
    _, act = end(*begin(act), g_in)
    grad_in = bf16(total[:32] + move(total[32:], "yh"))
    grad_w_in = lax.dot_general(
        toks.reshape(1024, 1024), slopes, (((0,), (0,)), ((), ())), preferred_element_type=jnp.float32
    )
    grad_w_out = lax.dot_general(
        act, grads.reshape(1024, 1024), (((0,), (0,)), ((), ())), preferred_element_type=jnp.float32
    )
    return (grad_in, grad_w_in * scale, grad_w_out * scale)


def solution(mesh):
    fine = Mesh(mesh.devices.reshape(8, 2, 2, 4, 2), DP + NODE)
    in_specs = (P(DP, NODE), P(DP, NODE), P(NODE, DP), P(DP, NODE))
    out_specs = (P(DP, NODE), P(NODE, DP), P(DP, NODE))
    return jax.shard_map(body, mesh=fine, in_specs=in_specs, out_specs=out_specs, check_vma=False)
```
